32 devices in a mesh: ind: 4 (over z), blk: 8 (over y, x, core).
Axes of the slice: x: 2, y: 2, z: 4, core: 2. Of those that a mesh axis runs over, the one named last changes fastest.
Arguments:
- genotypes: int32 [256, 16384], P('ind', 'blk'), may hold values from 0 to 2, as said below
- block_units: int32 [16], replicated, may hold values from 4 to 32, as said below
- sketch_seed: int32 [1], replicated, may hold values from 0 to 999999
Outputs:
- basis: float32 [16384, 256], P(('blk', 'ind'))
The draws below stay inside these ranges and needn't reach their ends.
Inputs may be any that keep to these rules, and one draw needn't show every extreme that they name: `block_units`: every block holds between 4 and 32 units; the units of all blocks sum to 128; one block holds exactly 32 and some hold exactly 4. `genotypes`: dosages are 0, 1 or 2.
All inputs are finite; a program needn't handle non-finite values.
Results may differ from the reference program's by a relative error of at most 0.0041.
Values sent between devices are 32-bit elements; how exact they have to be, the bound alone decides.
A program may use at most 64 MiB of HBM per device.

```python
import jax
import jax.numpy as jnp
from jax import lax

K = 256
UNIT = 128
NIND = 256
NSNP = 16384
NBLK = 16


def draw_genotypes(key, part):
    subkeys = jax.random.split(key, 2)
    permille = jax.random.randint(subkeys[0], (1, NSNP), 50, 501)
    paired = jax.random.randint(subkeys[1], (NIND, NSNP), 0, 1000000)
    first_allele = (paired // 1000 < permille).astype(jnp.int32)
    second_allele = (paired % 1000 < permille).astype(jnp.int32)
    return first_allele + second_allele


def draw_block_units(key, part):
    subkeys = jax.random.split(key, 2)
    others = NBLK - 6
    extra_total = 4 * NBLK - 48
    profile = [entry_id * 2 * extra_total // (others * others) for entry_id in range(others)]
    remaining = extra_total - sum(profile)
    position = others - 1
    while remaining > 0:
        profile[position] = profile[position] + 1
        remaining = remaining - 1
        position = position - 1 if position > 1 else others - 1
    size_pool = jnp.array([32] + [4 + step_units for step_units in profile], dtype=jnp.int32)
    pool_count = NBLK - 5
    shuffled = size_pool[jax.random.permutation(subkeys[0], pool_count)]
    cut_at = jax.random.randint(subkeys[1], (), 0, pool_count + 1)
    pool_ids = jnp.arange(pool_count, dtype=jnp.int32)
    prefix_sum = jnp.sum(jnp.where(pool_ids < cut_at, shuffled, 0))
    adjuster = 4 + jnp.mod(-3 - prefix_sum, 16)
    final_units = 28 - adjuster
    places = jnp.arange(NBLK, dtype=jnp.int32)
    from_pool = jnp.where(places < cut_at, places, places - 4)
    from_pool = jnp.clip(from_pool, 0, pool_count - 1)
    block_sizes = shuffled[from_pool]
    block_sizes = jnp.where(places == cut_at, adjuster, block_sizes)
    block_sizes = jnp.where(jnp.logical_and(places > cut_at, places <= cut_at + 3), 4, block_sizes)
    block_sizes = jnp.where(places == NBLK - 1, final_units, block_sizes)
    return block_sizes.astype(jnp.int32)


def setup_inputs(seed: int = 0) -> dict:
    seeds = jax.random.split(jax.random.key(seed), 4)
    genotypes = draw_genotypes(jax.random.fold_in(seeds[3], 71), 0)
    block_units = draw_block_units(jax.random.fold_in(seeds[3], 71), 0)
    sketch_seed = jax.random.randint(seeds[2], (1,), 0, 1000000).astype(jnp.int32)
    return {"genotypes": genotypes, "block_units": block_units, "sketch_seed": sketch_seed}


SHRINKAGE = 0.25

def sketch_signs(columns, seed_value, lane_count):
    lane_ids = jnp.arange(lane_count, dtype=jnp.int32)
    hashed = columns[:, None] * lane_count + lane_ids[None, :]
    hashed = jnp.bitwise_xor(hashed, seed_value)
    hashed = hashed * 73244475
    hashed = jnp.bitwise_xor(hashed, jnp.right_shift(hashed, 16))
    hashed = hashed * 73244475
    hashed = jnp.bitwise_xor(hashed, jnp.right_shift(hashed, 16))
    parity = jnp.bitwise_and(jnp.right_shift(hashed, 5), 1)
    return (1 - 2 * parity).astype(jnp.float32)

def reference(genotypes, block_units, sketch_seed):
    dosage = genotypes.astype(jnp.float32)
    people = dosage.shape[0]
    average = lax.optimization_barrier(jnp.sum(dosage, 0)) / people
    spread_sq = lax.optimization_barrier(jnp.sum(dosage * dosage, 0)) / people - average * average
    standard = ((dosage - average) * lax.rsqrt(spread_sq + 1e-05)).astype(jnp.bfloat16)
    widths = block_units * UNIT
    block_ends = jnp.cumsum(widths, dtype=jnp.int32)
    block_starts = block_ends - widths
    tile_count = NSNP // UNIT
    tile_start = jnp.arange(tile_count, dtype=jnp.int32) * UNIT
    tile_block = lax.optimization_barrier(jnp.sum((tile_start[:, None] >= block_starts[None, :]).astype(jnp.int32), axis=1)).astype(jnp.int32) - 1
    seed_value = sketch_seed[0]

    def sketch_tile(running, tile_id):
        columns = tile_id * UNIT + jnp.arange(UNIT, dtype=jnp.int32)
        pieces = lax.dynamic_slice_in_dim(standard, tile_id * UNIT, UNIT, 1)
        sign_rows = sketch_signs(columns, seed_value, K).astype(jnp.bfloat16)
        block_id = tile_block[tile_id]
        return (running.at[block_id].add(jnp.dot(pieces.astype(jnp.float32), sign_rows.astype(jnp.float32), preferred_element_type=jnp.float32)), None)
    block_sums, _ = lax.scan(sketch_tile, jnp.zeros((NBLK, people, K), jnp.float32), jnp.arange(tile_count, dtype=jnp.int32))
    sketch = block_sums.astype(jnp.bfloat16)

    def rows_tile(gram_sums, tile_id):
        columns = tile_id * UNIT + jnp.arange(UNIT, dtype=jnp.int32)
        pieces = lax.dynamic_slice_in_dim(standard, tile_id * UNIT, UNIT, 1)
        sign_rows = sketch_signs(columns, seed_value, K)
        block_id = tile_block[tile_id]
        product = lax.dot_general(pieces.astype(jnp.float32), sketch[block_id].astype(jnp.float32), (((0,), (0,)), ((), ())), preferred_element_type=jnp.float32)
        projected = product * ((1.0 - SHRINKAGE) / people) + SHRINKAGE * sign_rows
        outer = lax.dot_general(projected.astype(jnp.float32), projected.astype(jnp.float32), (((0,), (0,)), ((), ())), precision=lax.Precision.HIGHEST, preferred_element_type=jnp.float32)
        return (gram_sums.at[block_id].add(outer), projected)
    gram_sums, projected_tiles = lax.scan(rows_tile, jnp.zeros((NBLK, K, K), jnp.float32), jnp.arange(tile_count, dtype=jnp.int32))
    gram_sums = gram_sums / widths.astype(jnp.float32)[:, None, None]
    factor = jnp.linalg.cholesky(gram_sums)

    def solve_tile(projected, block_id):
        return jax.scipy.linalg.solve_triangular(factor[block_id], projected.T, lower=True).T
    basis_rows = jax.vmap(solve_tile)(projected_tiles, tile_block)
    return basis_rows.reshape(NSNP, K)
```

```python
import functools

import jax
import jax.numpy as jnp
from jax import lax
from jax.experimental import pallas as pl
from jax.experimental.pallas import tpu as pltpu
from jax.sharding import PartitionSpec as P

K = 256
UNIT = 128
MAX_UNITS = 32
MIN_UNITS = 4
SHRINKAGE = 0.25
STEP = 32
TILE = 8
EXACT = lax.Precision.HIGHEST
MESH = pl.DeviceIdType.MESH
NT = (((1,), (1,)), ((), ()))
TN = (((0,), (0,)), ((), ()))


def dot(a, b, dims=(((1,), (0,)), ((), ())), precision=None):
    return lax.dot_general(a, b, dims, precision=precision, preferred_element_type=jnp.float32)


def sign_tile(first_column, count, seed):
    columns = first_column + lax.broadcasted_iota(jnp.int32, (count, K), 0)
    hashed = columns * K + lax.broadcasted_iota(jnp.int32, (count, K), 1)
    hashed = hashed ^ seed
    hashed = hashed * 73244475
    hashed = hashed ^ (hashed >> 16)
    hashed = hashed * 73244475
    hashed = hashed ^ (hashed >> 16)
    return (1 - 2 * ((hashed >> 5) & 1)).astype(jnp.float32)


def block_bounds(units_ref, points):
    starts = [jnp.int32(0) for _ in points]
    ends = [jnp.int32(2**30) for _ in points]
    edge = jnp.int32(0)
    for b in range(units_ref.shape[0]):
        edge = edge + units_ref[b] * UNIT
        starts = [jnp.where(edge <= p, edge, s) for s, p in zip(starts, points)]
        ends = [jnp.where(edge > p, jnp.minimum(e, edge), e) for e, p in zip(ends, points)]
    return list(zip(starts, ends))


def gram_kernel(
    ind_count, blk_count, slots, reach,
    gen_ref, units_ref, seed_ref, gram_ref, proj_ref,
    gbuf, std, sign, send, rin, inbound, local, omega, ysum,
    gen_send, gen_recv, far_send, far_recv, near_send, near_recv,
):
    me = lax.axis_index("ind")
    group = lax.axis_index("blk")
    rows, span = gen_ref.shape
    people = rows * ind_count
    own = span // ind_count
    base = group * span
    chunk = min(people, 256)

    barrier = pltpu.get_barrier_semaphore()
    expected = jnp.int32(ind_count - 1)
    for off in range(1, ind_count):
        pl.semaphore_signal(
            barrier, inc=1, device_id={"ind": lax.rem(me + off, ind_count)}, device_id_type=MESH
        )
    for d in range(1, reach + 1):
        for ok, peer in ((group - d >= 0, group - d), (group + d < blk_count, group + d)):
            expected = expected + ok.astype(jnp.int32)

            @pl.when(ok)
            def _():
                pl.semaphore_signal(barrier, inc=1, device_id={"blk": peer}, device_id_type=MESH)

    pl.semaphore_wait(barrier, expected)

    def gen_copy(off, slot):
        return pltpu.make_async_remote_copy(
            src_ref=gen_ref, dst_ref=gbuf.at[slot],
            send_sem=gen_send.at[off], recv_sem=gen_recv.at[off],
            device_id={"ind": lax.rem(me + off, ind_count)}, device_id_type=MESH,
        )

    for off in range(1, ind_count):
        gen_copy(off, me).start()
    gbuf[me] = gen_ref[...]

    seed = seed_ref[0]
    own_base = base + me * own
    points = [base, base + span - 1, own_base, own_base + own - 1]
    bounds = block_bounds(units_ref, points)
    head, tail = bounds[0], bounds[1]
    mine = bounds[2 : 2 + slots]

    def fill_sign(t, _):
        at = pl.multiple_of(t * 128, 128)
        sign[pl.ds(at, 128), :] = sign_tile(base + at, 128, seed).astype(jnp.bfloat16)
        return 0

    lax.fori_loop(0, span // 128, fill_sign, 0)

    for s in range(slots):
        start, end = mine[s]
        omega[s] = jnp.zeros((K, K), jnp.float32)

        def add_signs(t, _):
            at = start + t * 256
            kept = at + lax.broadcasted_iota(jnp.int32, (256, K), 0) < end
            piece = jnp.where(kept, sign_tile(at, 256, seed), 0.0).astype(jnp.bfloat16)
            omega[s] += dot(piece, piece, TN)
            return 0

        lax.fori_loop(0, MAX_UNITS * UNIT // 256, add_signs, 0)

    for off in range(1, ind_count):
        gen_copy(off, lax.rem(me + ind_count - off, ind_count)).wait_recv()

    def standardise(t, _):
        at = pl.multiple_of(t * 256, 256)
        dosage = gbuf[:, :, pl.ds(at, 256)].astype(jnp.float32).reshape(people, 256)
        average = jnp.sum(dosage, 0, keepdims=True) / people
        spread = jnp.sum(dosage * dosage, 0, keepdims=True) / people - average * average
        std[:, pl.ds(at, 256)] = ((dosage - average) * lax.rsqrt(spread + 1e-05)).astype(
            jnp.bfloat16
        )
        return 0

    lax.fori_loop(0, span // 256, standardise, 0)

    ids = base + lax.broadcasted_iota(jnp.int32, (1, span), 1)

    def masked(values, limits):
        kept = jnp.logical_and(ids >= limits[0], ids < limits[1])
        return values * kept.astype(jnp.float32).astype(jnp.bfloat16)

    def products(part, write):
        def one(j, _):
            at = pl.multiple_of(j * chunk, chunk)
            write(pl.ds(at, chunk), dot(part, std[pl.ds(at, chunk), :], NT))
            return 0

        lax.fori_loop(0, people // chunk, one, 0)
        write(pl.ds(people, K), dot(part, sign[...]))

    my_rows = std[pl.ds(pl.multiple_of(me * rows, rows), rows), :]
    for side, limits in enumerate((head, tail)):

        def write_side(where, value):
            send[side, :, where] = value

        products(masked(my_rows, limits), write_side)

    def far_copy(side, d, peer):
        slot = side * reach + d - 1
        return pltpu.make_async_remote_copy(
            src_ref=send.at[side], dst_ref=rin.at[slot],
            send_sem=far_send.at[slot], recv_sem=far_recv.at[slot],
            device_id={"blk": peer}, device_id_type=MESH,
        )

    def neighbours(side, d):
        lower = (group - d >= 0, jnp.maximum(group - d, 0))
        upper = (group + d < blk_count, jnp.minimum(group + d, blk_count - 1))
        return (lower, upper) if side == 0 else (upper, lower)

    far = [(side, d) for d in range(1, reach + 1) for side in (0, 1)]
    for side, d in far:
        (ok, peer), _ = neighbours(side, d)

        @pl.when(ok)
        def _():
            far_copy(side, d, peer).start()

    for s in range(slots):

        def one_rows(i, _):
            at = pl.multiple_of(i * chunk, chunk)

            def write_local(where, value):
                local[s, pl.ds(at, chunk), where] = value

            products(masked(std[pl.ds(at, chunk), :], mine[s]), write_local)
            return 0

        lax.fori_loop(0, people // chunk, one_rows, 0)

    for into in (0, 1):
        inbound[into, me] = jnp.zeros(inbound.shape[2:], jnp.float32)
    for side, d in far:
        _, (ok, peer) = neighbours(side, d)
        into = 1 - side
        reaches = (
            head[0] < base - (d - 1) * span if into == 0 else tail[1] > base + d * span
        )

        @pl.when(ok)
        def _():
            far_copy(side, d, peer).wait_recv()
            inbound[into, me] += jnp.where(reaches, rin[side * reach + d - 1], 0.0)

    def near_copy(into, off, slot):
        return pltpu.make_async_remote_copy(
            src_ref=inbound.at[into, me], dst_ref=inbound.at[into, slot],
            send_sem=near_send.at[into, off], recv_sem=near_recv.at[into, off],
            device_id={"ind": lax.rem(me + off, ind_count)}, device_id_type=MESH,
        )

    for into in (0, 1):
        for off in range(1, ind_count):
            near_copy(into, off, me).start()
    for into in (0, 1):
        for off in range(1, ind_count):
            near_copy(into, off, lax.rem(me + ind_count - off, ind_count)).wait_recv()

    scale = (1.0 - SHRINKAGE) / people
    own_at = pl.multiple_of(me * own, own)
    own_ids = own_base + lax.broadcasted_iota(jnp.int32, (own, 1), 0)
    per = chunk // rows
    for s in range(slots):
        start, end = mine[s]
        is_head = start == head[0]
        is_tail = start == tail[0]

        def add_in(i, _):
            at = pl.multiple_of(i * chunk, chunk)
            part = pl.ds(i * per, per)
            shape = (chunk, people + K)
            total = local[s, pl.ds(at, chunk), :]
            total = total + jnp.where(is_head, inbound[0, part].reshape(shape), 0.0)
            total = total + jnp.where(is_tail, inbound[1, part].reshape(shape), 0.0)
            local[s, pl.ds(at, chunk), :] = total
            ysum[pl.ds(at, chunk), :] = total[:, people:].astype(jnp.bfloat16).astype(jnp.float32)
            return 0

        lax.fori_loop(0, people // chunk, add_in, 0)
        gram_ref[s] = (SHRINKAGE * SHRINKAGE) * omega[s]

        def add_gram(i, _):
            at = pl.multiple_of(i * chunk, chunk)
            inner = dot(local[s, pl.ds(at, chunk), :people], ysum[...], precision=EXACT)
            now = ysum[pl.ds(at, chunk), :]
            inner = inner * (scale * scale) + local[s, pl.ds(at, chunk), people:] * (
                2.0 * SHRINKAGE * scale
            )
            gram_ref[s] += dot(now, inner, TN, EXACT)
            return 0

        lax.fori_loop(0, people // chunk, add_gram, 0)
        whole = gram_ref[s]
        gram_ref[s] = (whole + whole.T) * (0.5 / (end - start).astype(jnp.float32))
        rows_now = dot(
            std[:, pl.ds(own_at, own)], ysum[...].astype(jnp.bfloat16), TN
        ) * scale + SHRINKAGE * sign[pl.ds(own_at, own), :].astype(jnp.float32)
        kept = jnp.logical_and(own_ids >= start, own_ids < end)
        if slots == 2 and s == 1:
            kept = jnp.logical_and(kept, own_ids >= mine[0][1])
        proj_ref[s] = jnp.where(kept, rows_now, 0.0)

    for off in range(1, ind_count):
        gen_copy(off, me).wait_send()
        for into in (0, 1):
            near_copy(into, off, me).wait_send()
    for side, d in far:
        (ok, peer), _ = neighbours(side, d)

        @pl.when(ok)
        def _():
            far_copy(side, d, peer).wait_send()


def basis_kernel(slots, gram_ref, proj_ref, out_ref, aug):
    row8 = lax.broadcasted_iota(jnp.int32, (TILE, 128), 0)
    lane8 = lax.broadcasted_iota(jnp.int32, (TILE, 128), 1)
    for s in range(slots):
        aug[s, :, :K] = gram_ref[s]
        aug[s, :, K:] = (
            lax.broadcasted_iota(jnp.int32, (K, K), 0) == lax.broadcasted_iota(jnp.int32, (K, K), 1)
        ).astype(jnp.float32)
    tiles = STEP // TILE
    for r0 in range(0, K, STEP):
        o = r0 % 128
        e = (o + 64) % 128
        work = []
        for s in range(slots):
            full = aug[s, r0 : r0 + STEP, r0 - o : r0 - o + 128]
            inside = jnp.logical_and(lane8 >= o, lane8 < o + STEP)
            work.append(
                [
                    jnp.where(
                        inside,
                        full[i * TILE : (i + 1) * TILE],
                        (lane8 == e + row8 + i * TILE).astype(jnp.float32),
                    )
                    for i in range(tiles)
                ]
            )
        for p in range(tiles):
            cols = [
                [
                    [
                        None if i < p else jnp.broadcast_to(
                            work[s][i][:, o + p * TILE + q : o + p * TILE + q + 1], (TILE, 128)
                        )
                        for i in range(tiles)
                    ]
                    for q in range(TILE)
                ]
                for s in range(slots)
            ]
            for q in range(TILE):
                for s in range(slots):
                    w, c = work[s], cols[s]
                    inv = 1.0 / c[q][p][q : q + 1]
                    pivots = [w[p][q : q + 1] * inv] + [
                        c[n][p][q : q + 1] * inv for n in range(q + 1, TILE)
                    ]
                    for i in range(p, tiles):
                        m = c[q][i]
                        if i == p:
                            m = jnp.where(row8 > q, m, 0.0)
                        w[i] = w[i] - m * pivots[0]
                        for n in range(q + 1, TILE):
                            c[n][i] = c[n][i] - m * pivots[n - q]
        for s in range(slots):
            inverse = []
            for i in range(tiles):
                here = lane8 == o + row8 + i * TILE
                pivot = jnp.sum(jnp.where(here, work[s][i], 0.0), 1, keepdims=True)
                inverse.append(work[s][i] * lax.rsqrt(pivot))
            lower = jnp.concatenate(inverse, 0)[:, e : e + STEP]
            panel = dot(lower, aug[s, r0 : r0 + STEP, :], precision=EXACT)
            aug[s, r0 : r0 + STEP, :] = panel
            if r0 + STEP < K:
                aug[s, r0 + STEP :, :] -= dot(panel[:, r0 + STEP : K], panel, TN, EXACT)
    total = dot(proj_ref[0], aug[0, :, K:], NT, EXACT)
    for s in range(1, slots):
        total = total + dot(proj_ref[s], aug[s, :, K:], NT, EXACT)
    out_ref[...] = total


def on_device(genotypes, block_units, sketch_seed):
    ind_count = lax.axis_size("ind")
    blk_count = lax.axis_size("blk")
    rows, span = genotypes.shape
    people = rows * ind_count
    own = span // ind_count
    slots = (own // UNIT + MIN_UNITS - 2) // MIN_UNITS + 1
    reach = -(-(MAX_UNITS - 1) // (span // UNIT))
    vmem = pl.BlockSpec(memory_space=pltpu.VMEM)
    smem = pl.BlockSpec(memory_space=pltpu.SMEM)
    wide = people + K
    gram, proj = pl.pallas_call(
        functools.partial(gram_kernel, ind_count, blk_count, slots, reach),
        out_shape=(
            jax.ShapeDtypeStruct((slots, K, K), jnp.float32),
            jax.ShapeDtypeStruct((slots, own, K), jnp.float32),
        ),
        in_specs=[vmem, smem, smem],
        out_specs=(vmem, vmem),
        scratch_shapes=[
            pltpu.VMEM((ind_count, rows, span), jnp.int32),
            pltpu.VMEM((people, span), jnp.bfloat16),
            pltpu.VMEM((span, K), jnp.bfloat16),
            pltpu.VMEM((2, rows, wide), jnp.float32),
            pltpu.VMEM((2 * reach, rows, wide), jnp.float32),
            pltpu.VMEM((2, ind_count, rows, wide), jnp.float32),
            pltpu.VMEM((slots, people, wide), jnp.float32),
            pltpu.VMEM((slots, K, K), jnp.float32),
            pltpu.VMEM((people, K), jnp.float32),
            pltpu.SemaphoreType.DMA((ind_count,)),
            pltpu.SemaphoreType.DMA((ind_count,)),
            pltpu.SemaphoreType.DMA((2 * reach,)),
            pltpu.SemaphoreType.DMA((2 * reach,)),
            pltpu.SemaphoreType.DMA((2, ind_count)),
            pltpu.SemaphoreType.DMA((2, ind_count)),
        ],
        compiler_params=pltpu.CompilerParams(
            collective_id=0, has_side_effects=True, vmem_limit_bytes=56 * 2**20
        ),
    )(genotypes, block_units, sketch_seed)
    return pl.pallas_call(
        functools.partial(basis_kernel, slots),
        out_shape=jax.ShapeDtypeStruct((own, K), jnp.float32),
        in_specs=[vmem, vmem],
        out_specs=vmem,
        scratch_shapes=[pltpu.VMEM((slots, K, 2 * K), jnp.float32)],
        compiler_params=pltpu.CompilerParams(vmem_limit_bytes=32 * 2**20),
    )(gram, proj)


def solution(mesh):
    return jax.shard_map(
        on_device,
        mesh=mesh,
        in_specs=(P("ind", "blk"), P(), P()),
        out_specs=P(("blk", "ind"), None),
        check_vma=False,
    )
```

```python
import functools

import jax
import jax.numpy as jnp
from jax import lax
from jax.experimental import pallas as pl
from jax.experimental.pallas import tpu as pltpu
from jax.sharding import PartitionSpec as P

K = 256
UNIT = 128
MAX_UNITS = 32
MIN_UNITS = 4
SHRINKAGE = 0.25
STEP = 32
TILE = 8
EXACT = lax.Precision.HIGHEST
MESH = pl.DeviceIdType.MESH
NT = (((1,), (1,)), ((), ()))
TN = (((0,), (0,)), ((), ()))


def dot(a, b, dims=(((1,), (0,)), ((), ())), precision=None):
    return lax.dot_general(a, b, dims, precision=precision, preferred_element_type=jnp.float32)


def sign_tile(first_column, count, seed):
    columns = first_column + lax.broadcasted_iota(jnp.int32, (count, K), 0)
    hashed = columns * K + lax.broadcasted_iota(jnp.int32, (count, K), 1)
    hashed = hashed ^ seed
    hashed = hashed * 73244475
    hashed = hashed ^ (hashed >> 16)
    hashed = hashed * 73244475
    hashed = hashed ^ (hashed >> 16)
    return (1 - 2 * ((hashed >> 5) & 1)).astype(jnp.float32)


def block_bounds(units_ref, points):
    starts = [jnp.int32(0) for _ in points]
    ends = [jnp.int32(2**30) for _ in points]
    edge = jnp.int32(0)
    for b in range(units_ref.shape[0]):
        edge = edge + units_ref[b] * UNIT
        starts = [jnp.where(edge <= p, edge, s) for s, p in zip(starts, points)]
        ends = [jnp.where(edge > p, jnp.minimum(e, edge), e) for e, p in zip(ends, points)]
    return list(zip(starts, ends))


def gram_kernel(
    ind_count, blk_count, slots, reach,
    gen_ref, units_ref, seed_ref, gram_ref, proj_ref,
    gbuf, std, sign, send, rin, inbound, local, omega, ysum,
    gen_send, gen_recv, far_send, far_recv, near_send, near_recv,
):
    me = lax.axis_index("ind")
    group = lax.axis_index("blk")
    rows, span = gen_ref.shape
    people = rows * ind_count
    own = span // ind_count
    base = group * span
    chunk = min(people, 256)

    barrier = pltpu.get_barrier_semaphore()
    expected = jnp.int32(ind_count - 1)
    for off in range(1, ind_count):
        pl.semaphore_signal(
            barrier, inc=1, device_id={"ind": lax.rem(me + off, ind_count)}, device_id_type=MESH
        )
    for d in range(1, reach + 1):
        for ok, peer in ((group - d >= 0, group - d), (group + d < blk_count, group + d)):
            expected = expected + ok.astype(jnp.int32)

            @pl.when(ok)
            def _():
                pl.semaphore_signal(barrier, inc=1, device_id={"blk": peer}, device_id_type=MESH)

    pl.semaphore_wait(barrier, expected)

    last = ind_count - 1

    def gen_copy(way, off, slot):
        step = 1 if way == 0 else -1
        return pltpu.make_async_remote_copy(
            src_ref=gen_ref if off == 0 else gbuf.at[slot], dst_ref=gbuf.at[slot],
            send_sem=gen_send.at[way, off], recv_sem=gen_recv.at[way, off],
            device_id={"ind": jnp.clip(me + step, 0, last)}, device_id_type=MESH,
        )

    def line(way, off):
        slot = me - off if way == 0 else me + off
        here = me - off >= 0 if way == 0 else me + off <= last
        onward = me < last if way == 0 else me > 0
        return jnp.clip(slot, 0, last), here, jnp.logical_and(here, onward)

    for way in (0, 1):
        slot, _, onward = line(way, 0)

        @pl.when(onward)
        def _():
            gen_copy(way, 0, slot).start()

    gbuf[me] = gen_ref[...]

    seed = seed_ref[0]
    own_base = base + me * own
    points = [base, base + span - 1, own_base, own_base + own - 1]
    bounds = block_bounds(units_ref, points)
    head, tail = bounds[0], bounds[1]
    mine = bounds[2 : 2 + slots]

    def fill_sign(t, _):
        at = pl.multiple_of(t * 128, 128)
        sign[pl.ds(at, 128), :] = sign_tile(base + at, 128, seed).astype(jnp.bfloat16)
        return 0

    lax.fori_loop(0, span // 128, fill_sign, 0)

    for s in range(slots):
        start, end = mine[s]
        omega[s] = jnp.zeros((K, K), jnp.float32)

        def add_signs(t, _):
            at = start + t * 256
            kept = at + lax.broadcasted_iota(jnp.int32, (256, K), 0) < end
            piece = jnp.where(kept, sign_tile(at, 256, seed), 0.0).astype(jnp.bfloat16)
            omega[s] += dot(piece, piece, TN)
            return 0

        lax.fori_loop(0, MAX_UNITS * UNIT // 256, add_signs, 0)

    for off in range(1, ind_count):
        for way in (0, 1):
            slot, here, onward = line(way, off)

            @pl.when(here)
            def _():
                gen_copy(way, off - 1, slot).wait_recv()

            @pl.when(onward)
            def _():
                gen_copy(way, off, slot).start()

    def standardise(t, _):
        at = pl.multiple_of(t * 256, 256)
        dosage = gbuf[:, :, pl.ds(at, 256)].astype(jnp.float32).reshape(people, 256)
        average = jnp.sum(dosage, 0, keepdims=True) / people
        spread = jnp.sum(dosage * dosage, 0, keepdims=True) / people - average * average
        std[:, pl.ds(at, 256)] = ((dosage - average) * lax.rsqrt(spread + 1e-05)).astype(
            jnp.bfloat16
        )
        return 0

    lax.fori_loop(0, span // 256, standardise, 0)

    ids = base + lax.broadcasted_iota(jnp.int32, (1, span), 1)

    def masked(values, limits):
        kept = jnp.logical_and(ids >= limits[0], ids < limits[1])
        return values * kept.astype(jnp.float32).astype(jnp.bfloat16)

    def products(part, write):
        def one(j, _):
            at = pl.multiple_of(j * chunk, chunk)
            write(pl.ds(at, chunk), dot(part, std[pl.ds(at, chunk), :], NT))
            return 0

        lax.fori_loop(0, people // chunk, one, 0)
        write(pl.ds(people, K), dot(part, sign[...]))

    my_rows = std[pl.ds(pl.multiple_of(me * rows, rows), rows), :]
    for side, limits in enumerate((head, tail)):

        def write_side(where, value):
            send[side, :, where] = value

        products(masked(my_rows, limits), write_side)

    def far_copy(side, d, peer):
        slot = side * reach + d - 1
        return pltpu.make_async_remote_copy(
            src_ref=send.at[side], dst_ref=rin.at[slot],
            send_sem=far_send.at[slot], recv_sem=far_recv.at[slot],
            device_id={"blk": peer}, device_id_type=MESH,
        )

    def neighbours(side, d):
        lower = (group - d >= 0, jnp.maximum(group - d, 0))
        upper = (group + d < blk_count, jnp.minimum(group + d, blk_count - 1))
        return (lower, upper) if side == 0 else (upper, lower)

    far = [(side, d) for d in range(1, reach + 1) for side in (0, 1)]
    for side, d in far:
        (ok, peer), _ = neighbours(side, d)

        @pl.when(ok)
        def _():
            far_copy(side, d, peer).start()

    for s in range(slots):

        def one_rows(i, _):
            at = pl.multiple_of(i * chunk, chunk)

            def write_local(where, value):
                local[s, pl.ds(at, chunk), where] = value

            products(masked(std[pl.ds(at, chunk), :], mine[s]), write_local)
            return 0

        lax.fori_loop(0, people // chunk, one_rows, 0)

    for into in (0, 1):
        inbound[into, me] = jnp.zeros(inbound.shape[2:], jnp.float32)
    for side, d in far:
        _, (ok, peer) = neighbours(side, d)
        into = 1 - side
        reaches = (
            head[0] < base - (d - 1) * span if into == 0 else tail[1] > base + d * span
        )

        @pl.when(ok)
        def _():
            far_copy(side, d, peer).wait_recv()
            inbound[into, me] += jnp.where(reaches, rin[side * reach + d - 1], 0.0)

    def near_copy(into, off, slot):
        return pltpu.make_async_remote_copy(
            src_ref=inbound.at[into, me], dst_ref=inbound.at[into, slot],
            send_sem=near_send.at[into, off], recv_sem=near_recv.at[into, off],
            device_id={"ind": lax.rem(me + off, ind_count)}, device_id_type=MESH,
        )

    for into in (0, 1):
        for off in range(1, ind_count):
            near_copy(into, off, me).start()
    for into in (0, 1):
        for off in range(1, ind_count):
            near_copy(into, off, lax.rem(me + ind_count - off, ind_count)).wait_recv()

    scale = (1.0 - SHRINKAGE) / people
    own_at = pl.multiple_of(me * own, own)
    own_ids = own_base + lax.broadcasted_iota(jnp.int32, (own, 1), 0)
    per = chunk // rows
    for s in range(slots):
        start, end = mine[s]
        is_head = start == head[0]
        is_tail = start == tail[0]

        def add_in(i, _):
            at = pl.multiple_of(i * chunk, chunk)
            part = pl.ds(i * per, per)
            shape = (chunk, people + K)
            total = local[s, pl.ds(at, chunk), :]
            total = total + jnp.where(is_head, inbound[0, part].reshape(shape), 0.0)
            total = total + jnp.where(is_tail, inbound[1, part].reshape(shape), 0.0)
            local[s, pl.ds(at, chunk), :] = total
            ysum[pl.ds(at, chunk), :] = total[:, people:].astype(jnp.bfloat16).astype(jnp.float32)
            return 0

        lax.fori_loop(0, people // chunk, add_in, 0)
        gram_ref[s] = (SHRINKAGE * SHRINKAGE) * omega[s]

        def add_gram(i, _):
            at = pl.multiple_of(i * chunk, chunk)
            inner = dot(local[s, pl.ds(at, chunk), :people], ysum[...], precision=EXACT)
            now = ysum[pl.ds(at, chunk), :]
            inner = inner * (scale * scale) + local[s, pl.ds(at, chunk), people:] * (
                2.0 * SHRINKAGE * scale
            )
            gram_ref[s] += dot(now, inner, TN, EXACT)
            return 0

        lax.fori_loop(0, people // chunk, add_gram, 0)
        whole = gram_ref[s]
        gram_ref[s] = (whole + whole.T) * (0.5 / (end - start).astype(jnp.float32))
        rows_now = dot(
            std[:, pl.ds(own_at, own)], ysum[...].astype(jnp.bfloat16), TN
        ) * scale + SHRINKAGE * sign[pl.ds(own_at, own), :].astype(jnp.float32)
        kept = jnp.logical_and(own_ids >= start, own_ids < end)
        if slots == 2 and s == 1:
            kept = jnp.logical_and(kept, own_ids >= mine[0][1])
        proj_ref[s] = jnp.where(kept, rows_now, 0.0)

    for off in range(1, ind_count):
        for into in (0, 1):
            near_copy(into, off, me).wait_send()
    for off in range(ind_count - 1):
        for way in (0, 1):
            slot, _, onward = line(way, off)

            @pl.when(onward)
            def _():
                gen_copy(way, off, slot).wait_send()

    for side, d in far:
        (ok, peer), _ = neighbours(side, d)

        @pl.when(ok)
        def _():
            far_copy(side, d, peer).wait_send()


def basis_kernel(slots, gram_ref, proj_hbm, out_ref, aug, proj_ref, proj_sem):
    fetch = pltpu.make_async_copy(proj_hbm, proj_ref, proj_sem)
    fetch.start()
    row8 = lax.broadcasted_iota(jnp.int32, (TILE, 128), 0)
    lane8 = lax.broadcasted_iota(jnp.int32, (TILE, 128), 1)
    for s in range(slots):
        aug[s, :, :K] = gram_ref[s]
        aug[s, :, K:] = (
            lax.broadcasted_iota(jnp.int32, (K, K), 0) == lax.broadcasted_iota(jnp.int32, (K, K), 1)
        ).astype(jnp.float32)
    tiles = STEP // TILE
    for r0 in range(0, K, STEP):
        o = r0 % 128
        e = (o + 64) % 128
        work = []
        for s in range(slots):
            full = aug[s, r0 : r0 + STEP, r0 - o : r0 - o + 128]
            inside = jnp.logical_and(lane8 >= o, lane8 < o + STEP)
            work.append(
                [
                    jnp.where(
                        inside,
                        full[i * TILE : (i + 1) * TILE],
                        (lane8 == e + row8 + i * TILE).astype(jnp.float32),
                    )
                    for i in range(tiles)
                ]
            )
        for p in range(tiles):
            cols = [
                [
                    [
                        None if i < p else jnp.broadcast_to(
                            work[s][i][:, o + p * TILE + q : o + p * TILE + q + 1], (TILE, 128)
                        )
                        for i in range(tiles)
                    ]
                    for q in range(TILE)
                ]
                for s in range(slots)
            ]
            for q in range(TILE):
                for s in range(slots):
                    w, c = work[s], cols[s]
                    pivot = c[q][p][q : q + 1]
                    inv = pl.reciprocal(pivot, approx=True)
                    inv = inv * (2.0 - pivot * inv)
                    pivots = [w[p][q : q + 1] * inv] + [
                        c[n][p][q : q + 1] * inv for n in range(q + 1, TILE)
                    ]
                    for i in range(p, tiles):
                        m = c[q][i]
                        if i == p:
                            m = jnp.where(row8 > q, m, 0.0)
                        w[i] = w[i] - m * pivots[0]
                        for n in range(q + 1, TILE):
                            c[n][i] = c[n][i] - m * pivots[n - q]
        for s in range(slots):
            inverse = []
            for i in range(tiles):
                here = lane8 == o + row8 + i * TILE
                pivot = jnp.sum(jnp.where(here, work[s][i], 0.0), 1, keepdims=True)
                inverse.append(work[s][i] * lax.rsqrt(pivot))
            lower = jnp.concatenate(inverse, 0)[:, e : e + STEP]
            panel = dot(lower, aug[s, r0 : r0 + STEP, :], precision=EXACT)
            aug[s, r0 : r0 + STEP, :] = panel
            if r0 + STEP < K:
                aug[s, r0 + STEP :, :] -= dot(panel[:, r0 + STEP : K], panel, TN, EXACT)
    fetch.wait()
    total = dot(proj_ref[0], aug[0, :, K:], NT, EXACT)
    for s in range(1, slots):
        total = total + dot(proj_ref[s], aug[s, :, K:], NT, EXACT)
    out_ref[...] = total


def on_device(genotypes, block_units, sketch_seed):
    ind_count = lax.axis_size("ind")
    blk_count = lax.axis_size("blk")
    rows, span = genotypes.shape
    people = rows * ind_count
    own = span // ind_count
    slots = (own // UNIT + MIN_UNITS - 2) // MIN_UNITS + 1
    reach = -(-(MAX_UNITS - 1) // (span // UNIT))
    vmem = pl.BlockSpec(memory_space=pltpu.VMEM)
    smem = pl.BlockSpec(memory_space=pltpu.SMEM)
    wide = people + K
    gram, proj = pl.pallas_call(
        functools.partial(gram_kernel, ind_count, blk_count, slots, reach),
        out_shape=(
            jax.ShapeDtypeStruct((slots, K, K), jnp.float32),
            jax.ShapeDtypeStruct((slots, own, K), jnp.float32),
        ),
        in_specs=[vmem, smem, smem],
        out_specs=(vmem, vmem),
        scratch_shapes=[
            pltpu.VMEM((ind_count, rows, span), jnp.int32),
            pltpu.VMEM((people, span), jnp.bfloat16),
            pltpu.VMEM((span, K), jnp.bfloat16),
            pltpu.VMEM((2, rows, wide), jnp.float32),
            pltpu.VMEM((2 * reach, rows, wide), jnp.float32),
            pltpu.VMEM((2, ind_count, rows, wide), jnp.float32),
            pltpu.VMEM((slots, people, wide), jnp.float32),
            pltpu.VMEM((slots, K, K), jnp.float32),
            pltpu.VMEM((people, K), jnp.float32),
            pltpu.SemaphoreType.DMA((2, ind_count)),
            pltpu.SemaphoreType.DMA((2, ind_count)),
            pltpu.SemaphoreType.DMA((2 * reach,)),
            pltpu.SemaphoreType.DMA((2 * reach,)),
            pltpu.SemaphoreType.DMA((2, ind_count)),
            pltpu.SemaphoreType.DMA((2, ind_count)),
        ],
        compiler_params=pltpu.CompilerParams(
            collective_id=0, has_side_effects=True, vmem_limit_bytes=56 * 2**20
        ),
    )(genotypes, block_units, sketch_seed)
    return pl.pallas_call(
        functools.partial(basis_kernel, slots),
        out_shape=jax.ShapeDtypeStruct((own, K), jnp.float32),
        in_specs=[vmem, pl.BlockSpec(memory_space=pl.ANY)],
        out_specs=vmem,
        scratch_shapes=[
            pltpu.VMEM((slots, K, 2 * K), jnp.float32),
            pltpu.VMEM((slots, own, K), jnp.float32),
            pltpu.SemaphoreType.DMA(()),
        ],
        compiler_params=pltpu.CompilerParams(vmem_limit_bytes=32 * 2**20),
    )(gram, proj)


def solution(mesh):
    return jax.shard_map(
        on_device,
        mesh=mesh,
        in_specs=(P("ind", "blk"), P(), P()),
        out_specs=P(("blk", "ind"), None),
        check_vma=False,
    )
```

```python
import functools

import jax
import jax.numpy as jnp
from jax import lax
from jax.experimental import pallas as pl
from jax.experimental.pallas import tpu as pltpu
from jax.sharding import PartitionSpec as P

K = 256
UNIT = 128
MAX_UNITS = 32
MIN_UNITS = 4
SHRINKAGE = 0.25
STEP = 32
TILE = 8
EXACT = lax.Precision.HIGHEST
MESH = pl.DeviceIdType.MESH
NT = (((1,), (1,)), ((), ()))
TN = (((0,), (0,)), ((), ()))


def dot(a, b, dims=(((1,), (0,)), ((), ())), precision=None):
    return lax.dot_general(a, b, dims, precision=precision, preferred_element_type=jnp.float32)


def sign_tile(first_column, count, seed):
    columns = first_column + lax.broadcasted_iota(jnp.int32, (count, K), 0)
    hashed = columns * K + lax.broadcasted_iota(jnp.int32, (count, K), 1)
    hashed = hashed ^ seed
    hashed = hashed * 73244475
    hashed = hashed ^ (hashed >> 16)
    hashed = hashed * 73244475
    hashed = hashed ^ (hashed >> 16)
    return (1 - 2 * ((hashed >> 5) & 1)).astype(jnp.float32)


def block_bounds(units_ref, points):
    starts = [jnp.int32(0) for _ in points]
    ends = [jnp.int32(2**30) for _ in points]
    edge = jnp.int32(0)
    for b in range(units_ref.shape[0]):
        edge = edge + units_ref[b] * UNIT
        starts = [jnp.where(edge <= p, edge, s) for s, p in zip(starts, points)]
        ends = [jnp.where(edge > p, jnp.minimum(e, edge), e) for e, p in zip(ends, points)]
    return list(zip(starts, ends))


def gram_kernel(
    ind_count, blk_count, slots, reach,
    gen_ref, units_ref, seed_ref, gram_ref, proj_ref,
    gbuf, stat, moments, own_rows, std, sign, send, rin, inbound, local, omega, ysum,
    gen_send, gen_recv, stat_send, stat_recv, far_send, far_recv, near_send, near_recv,
):
    me = lax.axis_index("ind")
    group = lax.axis_index("blk")
    rows, span = gen_ref.shape
    people = rows * ind_count
    own = span // ind_count
    base = group * span
    chunk = min(people, 256)

    barrier = pltpu.get_barrier_semaphore()
    expected = jnp.int32(ind_count - 1)
    for off in range(1, ind_count):
        pl.semaphore_signal(
            barrier, inc=1, device_id={"ind": lax.rem(me + off, ind_count)}, device_id_type=MESH
        )
    for d in range(1, reach + 1):
        for ok, peer in ((group - d >= 0, group - d), (group + d < blk_count, group + d)):
            expected = expected + ok.astype(jnp.int32)

            @pl.when(ok)
            def _():
                pl.semaphore_signal(barrier, inc=1, device_id={"blk": peer}, device_id_type=MESH)

    pl.semaphore_wait(barrier, expected)

    last = ind_count - 1

    def add_up(t, _):
        where = pl.ds(pl.multiple_of(t * 256, 256), 256)
        dosage = gen_ref[:, where].astype(jnp.float32)
        stat[me, 0:1, where] = jnp.sum(dosage, 0, keepdims=True)
        stat[me, 1:2, where] = jnp.sum(dosage * dosage, 0, keepdims=True)
        return 0

    lax.fori_loop(0, span // 256, add_up, 0)

    def stat_copy(off, slot):
        return pltpu.make_async_remote_copy(
            src_ref=stat.at[me], dst_ref=stat.at[slot],
            send_sem=stat_send.at[off], recv_sem=stat_recv.at[off],
            device_id={"ind": lax.rem(me + off, ind_count)}, device_id_type=MESH,
        )

    for off in range(1, ind_count):
        stat_copy(off, me).start()

    def gen_copy(way, off, slot):
        step = 1 if way == 0 else -1
        return pltpu.make_async_remote_copy(
            src_ref=gen_ref if off == 0 else gbuf.at[slot], dst_ref=gbuf.at[slot],
            send_sem=gen_send.at[way, off], recv_sem=gen_recv.at[way, off],
            device_id={"ind": jnp.clip(me + step, 0, last)}, device_id_type=MESH,
        )

    def line(way, off):
        slot = me - off if way == 0 else me + off
        here = me - off >= 0 if way == 0 else me + off <= last
        onward = me < last if way == 0 else me > 0
        return jnp.clip(slot, 0, last), here, jnp.logical_and(here, onward)

    for way in (0, 1):
        slot, _, onward = line(way, 0)

        @pl.when(onward)
        def _():
            gen_copy(way, 0, slot).start()

    gbuf[me] = gen_ref[...]

    seed = seed_ref[0]
    own_base = base + me * own
    points = [base, base + span - 1, own_base, own_base + own - 1]
    bounds = block_bounds(units_ref, points)
    head, tail = bounds[0], bounds[1]
    mine = bounds[2 : 2 + slots]

    def fill_sign(t, _):
        at = pl.multiple_of(t * 128, 128)
        sign[pl.ds(at, 128), :] = sign_tile(base + at, 128, seed).astype(jnp.bfloat16)
        return 0

    lax.fori_loop(0, span // 128, fill_sign, 0)

    for off in range(1, ind_count):
        stat_copy(off, lax.rem(me + ind_count - off, ind_count)).wait_recv()
    sums = jnp.sum(stat[...], 0)
    average = sums[0:1] / people
    moments[0:1] = average
    moments[1:2] = lax.rsqrt(sums[1:2] / people - average * average + 1e-05)

    def standard(dosage, where):
        return ((dosage - moments[0:1, where]) * moments[1:2, where]).astype(jnp.bfloat16)

    def standardise_mine(t, _):
        where = pl.ds(pl.multiple_of(t * 256, 256), 256)
        own_rows[:, where] = standard(gen_ref[:, where].astype(jnp.float32), where)
        return 0

    lax.fori_loop(0, span // 256, standardise_mine, 0)

    ids = base + lax.broadcasted_iota(jnp.int32, (1, span), 1)

    def masked(values, limits):
        kept = jnp.logical_and(ids >= limits[0], ids < limits[1])
        return values * kept.astype(jnp.float32).astype(jnp.bfloat16)

    parts = (pl.ds(0, people), pl.ds(people, K))

    def far_copy(part, side, d, peer):
        slot = side * reach + d - 1
        return pltpu.make_async_remote_copy(
            src_ref=send.at[side, :, parts[part]], dst_ref=rin.at[slot, :, parts[part]],
            send_sem=far_send.at[part, slot], recv_sem=far_recv.at[part, slot],
            device_id={"blk": peer}, device_id_type=MESH,
        )

    def neighbours(side, d):
        lower = (group - d >= 0, jnp.maximum(group - d, 0))
        upper = (group + d < blk_count, jnp.minimum(group + d, blk_count - 1))
        return (lower, upper) if side == 0 else (upper, lower)

    far = [(side, d) for d in range(1, reach + 1) for side in (0, 1)]

    def far_start(part):
        for side, d in far:
            (ok, peer), _ = neighbours(side, d)

            @pl.when(ok)
            def _():
                far_copy(part, side, d, peer).start()

    def near_copy(part, into, off, slot):
        return pltpu.make_async_remote_copy(
            src_ref=inbound.at[into, me, :, parts[part]],
            dst_ref=inbound.at[into, slot, :, parts[part]],
            send_sem=near_send.at[part * 2 + into, off],
            recv_sem=near_recv.at[part * 2 + into, off],
            device_id={"ind": lax.rem(me + off, ind_count)}, device_id_type=MESH,
        )

    def far_finish(part):
        where = parts[part]
        for into in (0, 1):
            inbound[into, me, :, where] = jnp.zeros((rows, where.size), jnp.float32)
        for side, d in far:
            _, (ok, peer) = neighbours(side, d)
            into = 1 - side
            reaches = (
                head[0] < base - (d - 1) * span if into == 0 else tail[1] > base + d * span
            )

            @pl.when(ok)
            def _():
                far_copy(part, side, d, peer).wait_recv()
                inbound[into, me, :, where] += jnp.where(
                    reaches, rin[side * reach + d - 1, :, where], 0.0
                )

        for into in (0, 1):
            for off in range(1, ind_count):
                near_copy(part, into, off, me).start()

    for side, limits in enumerate((head, tail)):
        send[side, :, parts[1]] = dot(masked(own_rows[...], limits), sign[...])
    far_start(1)

    for s in range(slots):
        start, end = mine[s]
        omega[s] = jnp.zeros((K, K), jnp.float32)

        def add_signs(t, _):
            at = start + t * 256
            kept = at + lax.broadcasted_iota(jnp.int32, (256, K), 0) < end
            piece = jnp.where(kept, sign_tile(at, 256, seed), 0.0).astype(jnp.bfloat16)
            omega[s] += dot(piece, piece, TN)
            return 0

        lax.fori_loop(0, MAX_UNITS * UNIT // 256, add_signs, 0)

    for off in range(1, ind_count):
        if off == min(2, ind_count - 1):
            far_finish(1)
        for way in (0, 1):
            slot, here, onward = line(way, off)

            @pl.when(here)
            def _():
                gen_copy(way, off - 1, slot).wait_recv()

            @pl.when(onward)
            def _():
                gen_copy(way, off, slot).start()

    def standardise(t, _):
        where = pl.ds(pl.multiple_of(t * 256, 256), 256)
        dosage = gbuf[:, :, where].astype(jnp.float32).reshape(people, 256)
        std[:, where] = standard(dosage, where)
        return 0

    lax.fori_loop(0, span // 256, standardise, 0)

    def products(part, write):
        def one(j, _):
            at = pl.multiple_of(j * chunk, chunk)
            write(pl.ds(at, chunk), dot(part, std[pl.ds(at, chunk), :], NT))
            return 0

        lax.fori_loop(0, people // chunk, one, 0)

    for side, limits in enumerate((head, tail)):

        def write_side(where, value):
            send[side, :, where] = value

        products(masked(own_rows[...], limits), write_side)
    far_start(0)

    for s in range(slots):

        def one_rows(i, _):
            at = pl.multiple_of(i * chunk, chunk)

            def write_local(where, value):
                local[s, pl.ds(at, chunk), where] = value

            now = masked(std[pl.ds(at, chunk), :], mine[s])
            products(now, write_local)
            write_local(parts[1], dot(now, sign[...]))
            return 0

        lax.fori_loop(0, people // chunk, one_rows, 0)

    far_finish(0)
    for part in (1, 0):
        for into in (0, 1):
            for off in range(1, ind_count):
                slot = lax.rem(me + ind_count - off, ind_count)
                near_copy(part, into, off, slot).wait_recv()

    scale = (1.0 - SHRINKAGE) / people
    own_at = pl.multiple_of(me * own, own)
    own_ids = own_base + lax.broadcasted_iota(jnp.int32, (own, 1), 0)
    per = chunk // rows
    for s in range(slots):
        start, end = mine[s]
        is_head = start == head[0]
        is_tail = start == tail[0]

        def add_in(i, _):
            at = pl.multiple_of(i * chunk, chunk)
            part = pl.ds(i * per, per)
            shape = (chunk, people + K)
            total = local[s, pl.ds(at, chunk), :]
            total = total + jnp.where(is_head, inbound[0, part].reshape(shape), 0.0)
            total = total + jnp.where(is_tail, inbound[1, part].reshape(shape), 0.0)
            local[s, pl.ds(at, chunk), :] = total
            ysum[pl.ds(at, chunk), :] = total[:, people:].astype(jnp.bfloat16).astype(jnp.float32)
            return 0

        lax.fori_loop(0, people // chunk, add_in, 0)
        gram_ref[s] = (SHRINKAGE * SHRINKAGE) * omega[s]

        def add_gram(i, _):
            at = pl.multiple_of(i * chunk, chunk)
            inner = dot(local[s, pl.ds(at, chunk), :people], ysum[...], precision=EXACT)
            now = ysum[pl.ds(at, chunk), :]
            inner = inner * (scale * scale) + local[s, pl.ds(at, chunk), people:] * (
                2.0 * SHRINKAGE * scale
            )
            gram_ref[s] += dot(now, inner, TN, EXACT)
            return 0

        lax.fori_loop(0, people // chunk, add_gram, 0)
        whole = gram_ref[s]
        gram_ref[s] = (whole + whole.T) * (0.5 / (end - start).astype(jnp.float32))
        rows_now = dot(
            std[:, pl.ds(own_at, own)], ysum[...].astype(jnp.bfloat16), TN
        ) * scale + SHRINKAGE * sign[pl.ds(own_at, own), :].astype(jnp.float32)
        kept = jnp.logical_and(own_ids >= start, own_ids < end)
        if slots == 2 and s == 1:
            kept = jnp.logical_and(kept, own_ids >= mine[0][1])
        proj_ref[s] = jnp.where(kept, rows_now, 0.0)

    for off in range(1, ind_count):
        stat_copy(off, me).wait_send()
        for part in (0, 1):
            for into in (0, 1):
                near_copy(part, into, off, me).wait_send()
    for off in range(ind_count - 1):
        for way in (0, 1):
            slot, _, onward = line(way, off)

            @pl.when(onward)
            def _():
                gen_copy(way, off, slot).wait_send()

    for side, d in far:
        (ok, peer), _ = neighbours(side, d)

        @pl.when(ok)
        def _():
            for part in (0, 1):
                far_copy(part, side, d, peer).wait_send()


def basis_kernel(slots, gram_ref, proj_hbm, out_ref, aug, proj_ref, proj_sem):
    fetch = pltpu.make_async_copy(proj_hbm, proj_ref, proj_sem)
    fetch.start()
    row8 = lax.broadcasted_iota(jnp.int32, (TILE, 128), 0)
    lane8 = lax.broadcasted_iota(jnp.int32, (TILE, 128), 1)
    for s in range(slots):
        aug[s, :, :K] = gram_ref[s]
        aug[s, :, K:] = (
            lax.broadcasted_iota(jnp.int32, (K, K), 0) == lax.broadcasted_iota(jnp.int32, (K, K), 1)
        ).astype(jnp.float32)
    tiles = STEP // TILE
    for r0 in range(0, K, STEP):
        o = r0 % 128
        e = (o + 64) % 128
        work = []
        for s in range(slots):
            full = aug[s, r0 : r0 + STEP, r0 - o : r0 - o + 128]
            inside = jnp.logical_and(lane8 >= o, lane8 < o + STEP)
            work.append(
                [
                    jnp.where(
                        inside,
                        full[i * TILE : (i + 1) * TILE],
                        (lane8 == e + row8 + i * TILE).astype(jnp.float32),
                    )
                    for i in range(tiles)
                ]
            )
        for p in range(tiles):
            cols = [
                [
                    [
                        None if i < p else jnp.broadcast_to(
                            work[s][i][:, o + p * TILE + q : o + p * TILE + q + 1], (TILE, 128)
                        )
                        for i in range(tiles)
                    ]
                    for q in range(TILE)
                ]
                for s in range(slots)
            ]
            for q in range(TILE):
                for s in range(slots):
                    w, c = work[s], cols[s]
                    pivot = c[q][p][q : q + 1]
                    inv = pl.reciprocal(pivot, approx=True)
                    inv = inv * (2.0 - pivot * inv)
                    pivots = [w[p][q : q + 1] * inv] + [
                        c[n][p][q : q + 1] * inv for n in range(q + 1, TILE)
                    ]
                    for i in range(p, tiles):
                        m = c[q][i]
                        if i == p:
                            m = jnp.where(row8 > q, m, 0.0)
                        w[i] = w[i] - m * pivots[0]
                        for n in range(q + 1, TILE):
                            c[n][i] = c[n][i] - m * pivots[n - q]
        for s in range(slots):
            inverse = []
            for i in range(tiles):
                here = lane8 == o + row8 + i * TILE
                pivot = jnp.sum(jnp.where(here, work[s][i], 0.0), 1, keepdims=True)
                inverse.append(work[s][i] * lax.rsqrt(pivot))
            lower = jnp.concatenate(inverse, 0)[:, e : e + STEP]
            panel = dot(lower, aug[s, r0 : r0 + STEP, :], precision=EXACT)
            aug[s, r0 : r0 + STEP, :] = panel
            if r0 + STEP < K:
                aug[s, r0 + STEP :, :] -= dot(panel[:, r0 + STEP : K], panel, TN, EXACT)
    fetch.wait()
    total = dot(proj_ref[0], aug[0, :, K:], NT, EXACT)
    for s in range(1, slots):
        total = total + dot(proj_ref[s], aug[s, :, K:], NT, EXACT)
    out_ref[...] = total


def on_device(genotypes, block_units, sketch_seed):
    ind_count = lax.axis_size("ind")
    blk_count = lax.axis_size("blk")
    rows, span = genotypes.shape
    people = rows * ind_count
    own = span // ind_count
    slots = (own // UNIT + MIN_UNITS - 2) // MIN_UNITS + 1
    reach = -(-(MAX_UNITS - 1) // (span // UNIT))
    vmem = pl.BlockSpec(memory_space=pltpu.VMEM)
    smem = pl.BlockSpec(memory_space=pltpu.SMEM)
    wide = people + K
    gram, proj = pl.pallas_call(
        functools.partial(gram_kernel, ind_count, blk_count, slots, reach),
        out_shape=(
            jax.ShapeDtypeStruct((slots, K, K), jnp.float32),
            jax.ShapeDtypeStruct((slots, own, K), jnp.float32),
        ),
        in_specs=[vmem, smem, smem],
        out_specs=(vmem, vmem),
        scratch_shapes=[
            pltpu.VMEM((ind_count, rows, span), jnp.int32),
            pltpu.VMEM((ind_count, 2, span), jnp.float32),
            pltpu.VMEM((2, span), jnp.float32),
            pltpu.VMEM((rows, span), jnp.bfloat16),
            pltpu.VMEM((people, span), jnp.bfloat16),
            pltpu.VMEM((span, K), jnp.bfloat16),
            pltpu.VMEM((2, rows, wide), jnp.float32),
            pltpu.VMEM((2 * reach, rows, wide), jnp.float32),
            pltpu.VMEM((2, ind_count, rows, wide), jnp.float32),
            pltpu.VMEM((slots, people, wide), jnp.float32),
            pltpu.VMEM((slots, K, K), jnp.float32),
            pltpu.VMEM((people, K), jnp.float32),
            pltpu.SemaphoreType.DMA((2, ind_count)),
            pltpu.SemaphoreType.DMA((2, ind_count)),
            pltpu.SemaphoreType.DMA((ind_count,)),
            pltpu.SemaphoreType.DMA((ind_count,)),
            pltpu.SemaphoreType.DMA((2, 2 * reach)),
            pltpu.SemaphoreType.DMA((2, 2 * reach)),
            pltpu.SemaphoreType.DMA((4, ind_count)),
            pltpu.SemaphoreType.DMA((4, ind_count)),
        ],
        compiler_params=pltpu.CompilerParams(
            collective_id=0, has_side_effects=True, vmem_limit_bytes=56 * 2**20
        ),
    )(genotypes, block_units, sketch_seed)
    return pl.pallas_call(
        functools.partial(basis_kernel, slots),
        out_shape=jax.ShapeDtypeStruct((own, K), jnp.float32),
        in_specs=[vmem, pl.BlockSpec(memory_space=pl.ANY)],
        out_specs=vmem,
        scratch_shapes=[
            pltpu.VMEM((slots, K, 2 * K), jnp.float32),
            pltpu.VMEM((slots, own, K), jnp.float32),
            pltpu.SemaphoreType.DMA(()),
        ],
        compiler_params=pltpu.CompilerParams(vmem_limit_bytes=60 * 2**20),
    )(gram, proj)


def solution(mesh):
    return jax.shard_map(
        on_device,
        mesh=mesh,
        in_specs=(P("ind", "blk"), P(), P()),
        out_specs=P(("blk", "ind"), None),
        check_vma=False,
    )
```

```python
import functools

import jax
import jax.numpy as jnp
from jax import lax
from jax.experimental import pallas as pl
from jax.experimental.pallas import tpu as pltpu
from jax.sharding import PartitionSpec as P

K = 256
UNIT = 128
MAX_UNITS = 32
MIN_UNITS = 4
SHRINKAGE = 0.25
STEP = 32
TILE = 8
EXACT = lax.Precision.HIGHEST
MESH = pl.DeviceIdType.MESH
NT = (((1,), (1,)), ((), ()))
TN = (((0,), (0,)), ((), ()))


def dot(a, b, dims=(((1,), (0,)), ((), ())), precision=None):
    return lax.dot_general(a, b, dims, precision=precision, preferred_element_type=jnp.float32)


def sign_tile(first_column, count, seed):
    columns = first_column + lax.broadcasted_iota(jnp.int32, (count, K), 0)
    hashed = columns * K + lax.broadcasted_iota(jnp.int32, (count, K), 1)
    hashed = hashed ^ seed
    hashed = hashed * 73244475
    hashed = hashed ^ (hashed >> 16)
    hashed = hashed * 73244475
    hashed = hashed ^ (hashed >> 16)
    return (1 - 2 * ((hashed >> 5) & 1)).astype(jnp.float32)


def block_bounds(units_ref, points):
    starts = [jnp.int32(0) for _ in points]
    ends = [jnp.int32(2**30) for _ in points]
    edge = jnp.int32(0)
    for b in range(units_ref.shape[0]):
        edge = edge + units_ref[b] * UNIT
        starts = [jnp.where(edge <= p, edge, s) for s, p in zip(starts, points)]
        ends = [jnp.where(edge > p, jnp.minimum(e, edge), e) for e, p in zip(ends, points)]
    return list(zip(starts, ends))


def gram_kernel(
    ind_count, blk_count, slots, reach,
    gen_ref, units_ref, seed_ref, gram_ref, proj_ref,
    gbuf, stat, moments, own_rows, std, sign, send, rin, inbound, local, omega, ysum,
    gen_send, gen_recv, stat_send, stat_recv, far_send, far_recv, near_send, near_recv,
):
    me = lax.axis_index("ind")
    group = lax.axis_index("blk")
    rows, span = gen_ref.shape
    people = rows * ind_count
    own = span // ind_count
    base = group * span
    chunk = min(people, 256)

    barrier = pltpu.get_barrier_semaphore()
    expected = jnp.int32(ind_count - 1)
    for off in range(1, ind_count):
        pl.semaphore_signal(
            barrier, inc=1, device_id={"ind": lax.rem(me + off, ind_count)}, device_id_type=MESH
        )
    for d in range(1, reach + 1):
        for ok, peer in ((group - d >= 0, group - d), (group + d < blk_count, group + d)):
            expected = expected + ok.astype(jnp.int32)

            @pl.when(ok)
            def _():
                pl.semaphore_signal(barrier, inc=1, device_id={"blk": peer}, device_id_type=MESH)

    pl.semaphore_wait(barrier, expected)

    last = ind_count - 1

    def add_up(t, _):
        where = pl.ds(pl.multiple_of(t * 256, 256), 256)
        dosage = gen_ref[:, where].astype(jnp.float32)
        stat[me, 0:1, where] = jnp.sum(dosage, 0, keepdims=True)
        stat[me, 1:2, where] = jnp.sum(dosage * dosage, 0, keepdims=True)
        return 0

    lax.fori_loop(0, span // 256, add_up, 0)

    def stat_copy(off, slot):
        return pltpu.make_async_remote_copy(
            src_ref=stat.at[me], dst_ref=stat.at[slot],
            send_sem=stat_send.at[off], recv_sem=stat_recv.at[off],
            device_id={"ind": lax.rem(me + off, ind_count)}, device_id_type=MESH,
        )

    for off in range(1, ind_count):
        stat_copy(off, me).start()

    def gen_copy(way, off, slot):
        step = 1 if way == 0 else -1
        return pltpu.make_async_remote_copy(
            src_ref=gen_ref if off == 0 else gbuf.at[slot], dst_ref=gbuf.at[slot],
            send_sem=gen_send.at[way, off], recv_sem=gen_recv.at[way, off],
            device_id={"ind": jnp.clip(me + step, 0, last)}, device_id_type=MESH,
        )

    def line(way, off):
        slot = me - off if way == 0 else me + off
        here = me - off >= 0 if way == 0 else me + off <= last
        onward = me < last if way == 0 else me > 0
        return jnp.clip(slot, 0, last), here, jnp.logical_and(here, onward)

    for way in (0, 1):
        slot, _, onward = line(way, 0)

        @pl.when(onward)
        def _():
            gen_copy(way, 0, slot).start()

    gbuf[me] = gen_ref[...]

    seed = seed_ref[0]
    own_base = base + me * own
    points = [base, base + span - 1, own_base, own_base + own - 1]
    bounds = block_bounds(units_ref, points)
    head, tail = bounds[0], bounds[1]
    mine = bounds[2 : 2 + slots]

    def fill_sign(t, _):
        at = pl.multiple_of(t * 128, 128)
        sign[pl.ds(at, 128), :] = sign_tile(base + at, 128, seed).astype(jnp.bfloat16)
        return 0

    lax.fori_loop(0, span // 128, fill_sign, 0)

    for off in range(1, ind_count):
        stat_copy(off, lax.rem(me + ind_count - off, ind_count)).wait_recv()
    sums = jnp.sum(stat[...], 0)
    average = sums[0:1] / people
    moments[0:1] = average
    moments[1:2] = lax.rsqrt(sums[1:2] / people - average * average + 1e-05)

    def standard(dosage, where):
        return ((dosage - moments[0:1, where]) * moments[1:2, where]).astype(jnp.bfloat16)

    def standardise_mine(t, _):
        where = pl.ds(pl.multiple_of(t * 256, 256), 256)
        own_rows[:, where] = standard(gen_ref[:, where].astype(jnp.float32), where)
        return 0

    lax.fori_loop(0, span // 256, standardise_mine, 0)

    ids = base + lax.broadcasted_iota(jnp.int32, (1, span), 1)

    def masked(values, limits):
        kept = jnp.logical_and(ids >= limits[0], ids < limits[1])
        return values * kept.astype(jnp.float32).astype(jnp.bfloat16)

    parts = (pl.ds(0, people), pl.ds(people, K))

    def far_copy(part, side, d, peer):
        slot = side * reach + d - 1
        return pltpu.make_async_remote_copy(
            src_ref=send.at[side, :, parts[part]], dst_ref=rin.at[slot, :, parts[part]],
            send_sem=far_send.at[part, slot], recv_sem=far_recv.at[part, slot],
            device_id={"blk": peer}, device_id_type=MESH,
        )

    def neighbours(side, d):
        lower = (group - d >= 0, jnp.maximum(group - d, 0))
        upper = (group + d < blk_count, jnp.minimum(group + d, blk_count - 1))
        return (lower, upper) if side == 0 else (upper, lower)

    far = [(side, d) for d in range(1, reach + 1) for side in (0, 1)]

    def far_start(part):
        for side, d in far:
            (ok, peer), _ = neighbours(side, d)

            @pl.when(ok)
            def _():
                far_copy(part, side, d, peer).start()

    def near_copy(part, into, off, slot):
        return pltpu.make_async_remote_copy(
            src_ref=inbound.at[into, me, :, parts[part]],
            dst_ref=inbound.at[into, slot, :, parts[part]],
            send_sem=near_send.at[part * 2 + into, off],
            recv_sem=near_recv.at[part * 2 + into, off],
            device_id={"ind": lax.rem(me + off, ind_count)}, device_id_type=MESH,
        )

    def far_finish(part):
        where = parts[part]
        for into in (0, 1):
            inbound[into, me, :, where] = jnp.zeros((rows, where.size), jnp.float32)
        for side, d in far:
            _, (ok, peer) = neighbours(side, d)
            into = 1 - side
            reaches = (
                head[0] < base - (d - 1) * span if into == 0 else tail[1] > base + d * span
            )

            @pl.when(ok)
            def _():
                far_copy(part, side, d, peer).wait_recv()
                inbound[into, me, :, where] += jnp.where(
                    reaches, rin[side * reach + d - 1, :, where], 0.0
                )

        for into in (0, 1):
            for off in range(1, ind_count):
                near_copy(part, into, off, me).start()

    for side, limits in enumerate((head, tail)):
        send[side, :, parts[1]] = dot(masked(own_rows[...], limits), sign[...])
    far_start(1)

    for s in range(slots):
        start, end = mine[s]
        omega[s] = jnp.zeros((K, K), jnp.float32)

        def add_signs(t, _):
            at = start + t * 256
            kept = at + lax.broadcasted_iota(jnp.int32, (256, K), 0) < end
            piece = jnp.where(kept, sign_tile(at, 256, seed), 0.0).astype(jnp.bfloat16)
            omega[s] += dot(piece, piece, TN)
            return 0

        lax.fori_loop(0, MAX_UNITS * UNIT // 256, add_signs, 0)

    for off in range(1, ind_count):
        if off == min(2, ind_count - 1):
            far_finish(1)
        for way in (0, 1):
            slot, here, onward = line(way, off)

            @pl.when(here)
            def _():
                gen_copy(way, off - 1, slot).wait_recv()

            @pl.when(onward)
            def _():
                gen_copy(way, off, slot).start()

    def standardise(t, _):
        where = pl.ds(pl.multiple_of(t * 256, 256), 256)
        dosage = gbuf[:, :, where].astype(jnp.float32).reshape(people, 256)
        std[:, where] = standard(dosage, where)
        return 0

    lax.fori_loop(0, span // 256, standardise, 0)

    def products(part, write):
        def one(j, _):
            at = pl.multiple_of(j * chunk, chunk)
            write(pl.ds(at, chunk), dot(part, std[pl.ds(at, chunk), :], NT))
            return 0

        lax.fori_loop(0, people // chunk, one, 0)

    for side, limits in enumerate((head, tail)):

        def write_side(where, value):
            send[side, :, where] = value

        products(masked(own_rows[...], limits), write_side)
    far_start(0)

    for s in range(slots):

        def one_rows(i, _):
            at = pl.multiple_of(i * chunk, chunk)

            def write_local(where, value):
                local[s, pl.ds(at, chunk), where] = value

            now = masked(std[pl.ds(at, chunk), :], mine[s])
            products(now, write_local)
            write_local(parts[1], dot(now, sign[...]))
            return 0

        lax.fori_loop(0, people // chunk, one_rows, 0)

    far_finish(0)

    def near_finish(part):
        for into in (0, 1):
            for off in range(1, ind_count):
                slot = lax.rem(me + ind_count - off, ind_count)
                near_copy(part, into, off, slot).wait_recv()

    scale = (1.0 - SHRINKAGE) / people
    own_at = pl.multiple_of(me * own, own)
    own_ids = own_base + lax.broadcasted_iota(jnp.int32, (own, 1), 0)
    per = chunk // rows

    def add_in(s, part):
        where = parts[part]

        def one(i, _):
            at = pl.multiple_of(i * chunk, chunk)
            heap = pl.ds(i * per, per)
            shape = (chunk, where.size)
            is_head, is_tail = mine[s][0] == head[0], mine[s][0] == tail[0]
            total = local[s, pl.ds(at, chunk), where]
            total = total + jnp.where(is_head, inbound[0, heap, :, where].reshape(shape), 0.0)
            total = total + jnp.where(is_tail, inbound[1, heap, :, where].reshape(shape), 0.0)
            local[s, pl.ds(at, chunk), where] = total
            if part == 1:
                ysum[s, pl.ds(at, chunk), :] = total.astype(jnp.bfloat16).astype(jnp.float32)
            return 0

        lax.fori_loop(0, people // chunk, one, 0)

    near_finish(1)
    for s in range(slots):
        start, end = mine[s]
        add_in(s, 1)
        rows_now = dot(
            std[:, pl.ds(own_at, own)], ysum[s].astype(jnp.bfloat16), TN
        ) * scale + SHRINKAGE * sign[pl.ds(own_at, own), :].astype(jnp.float32)
        kept = jnp.logical_and(own_ids >= start, own_ids < end)
        if slots == 2 and s == 1:
            kept = jnp.logical_and(kept, own_ids >= mine[0][1])
        proj_ref[s] = jnp.where(kept, rows_now, 0.0)

    near_finish(0)
    for s in range(slots):
        start, end = mine[s]
        add_in(s, 0)
        gram_ref[s] = (SHRINKAGE * SHRINKAGE) * omega[s]

        def add_gram(i, _):
            at = pl.multiple_of(i * chunk, chunk)
            inner = dot(local[s, pl.ds(at, chunk), :people], ysum[s], precision=EXACT)
            inner = inner * (scale * scale) + local[s, pl.ds(at, chunk), people:] * (
                2.0 * SHRINKAGE * scale
            )
            gram_ref[s] += dot(ysum[s, pl.ds(at, chunk), :], inner, TN, EXACT)
            return 0

        lax.fori_loop(0, people // chunk, add_gram, 0)
        whole = gram_ref[s]
        gram_ref[s] = (whole + whole.T) * (0.5 / (end - start).astype(jnp.float32))

    for off in range(1, ind_count):
        stat_copy(off, me).wait_send()
        for part in (0, 1):
            for into in (0, 1):
                near_copy(part, into, off, me).wait_send()
    for off in range(ind_count - 1):
        for way in (0, 1):
            slot, _, onward = line(way, off)

            @pl.when(onward)
            def _():
                gen_copy(way, off, slot).wait_send()

    for side, d in far:
        (ok, peer), _ = neighbours(side, d)

        @pl.when(ok)
        def _():
            for part in (0, 1):
                far_copy(part, side, d, peer).wait_send()


def basis_kernel(slots, gram_ref, proj_hbm, out_ref, aug, proj_ref, proj_sem):
    fetch = pltpu.make_async_copy(proj_hbm, proj_ref, proj_sem)
    fetch.start()
    row8 = lax.broadcasted_iota(jnp.int32, (TILE, 128), 0)
    lane8 = lax.broadcasted_iota(jnp.int32, (TILE, 128), 1)
    for s in range(slots):
        aug[s, :, :K] = gram_ref[s]
        aug[s, :, K:] = (
            lax.broadcasted_iota(jnp.int32, (K, K), 0) == lax.broadcasted_iota(jnp.int32, (K, K), 1)
        ).astype(jnp.float32)
    tiles = STEP // TILE
    for r0 in range(0, K, STEP):
        o = r0 % 128
        e = (o + 64) % 128
        work = []
        for s in range(slots):
            full = aug[s, r0 : r0 + STEP, r0 - o : r0 - o + 128]
            inside = jnp.logical_and(lane8 >= o, lane8 < o + STEP)
            work.append(
                [
                    jnp.where(
                        inside,
                        full[i * TILE : (i + 1) * TILE],
                        (lane8 == e + row8 + i * TILE).astype(jnp.float32),
                    )
                    for i in range(tiles)
                ]
            )
        for p in range(tiles):
            cols = [
                [
                    [
                        None if i < p else jnp.broadcast_to(
                            work[s][i][:, o + p * TILE + q : o + p * TILE + q + 1], (TILE, 128)
                        )
                        for i in range(tiles)
                    ]
                    for q in range(TILE)
                ]
                for s in range(slots)
            ]
            for q in range(TILE):
                for s in range(slots):
                    w, c = work[s], cols[s]
                    pivot = c[q][p][q : q + 1]
                    inv = pl.reciprocal(pivot, approx=True)
                    inv = inv * (2.0 - pivot * inv)
                    pivots = [w[p][q : q + 1] * inv] + [
                        c[n][p][q : q + 1] * inv for n in range(q + 1, TILE)
                    ]
                    for i in range(p, tiles):
                        m = c[q][i]
                        if i == p:
                            m = jnp.where(row8 > q, m, 0.0)
                        w[i] = w[i] - m * pivots[0]
                        for n in range(q + 1, TILE):
                            c[n][i] = c[n][i] - m * pivots[n - q]
        for s in range(slots):
            inverse = []
            for i in range(tiles):
                here = lane8 == o + row8 + i * TILE
                pivot = jnp.sum(jnp.where(here, work[s][i], 0.0), 1, keepdims=True)
                inverse.append(work[s][i] * lax.rsqrt(pivot))
            lower = jnp.concatenate(inverse, 0)[:, e : e + STEP]
            lo = r0 - o
            hi = K + lo + 128
            panel = dot(lower, aug[s, r0 : r0 + STEP, lo:hi], precision=EXACT)
            aug[s, r0 : r0 + STEP, lo:hi] = panel
            if r0 + STEP < K:
                aug[s, r0 + STEP :, lo:hi] -= dot(
                    panel[:, r0 + STEP - lo : K - lo], panel, TN, EXACT
                )
    fetch.wait()
    total = dot(proj_ref[0], aug[0, :, K:], NT, EXACT)
    for s in range(1, slots):
        total = total + dot(proj_ref[s], aug[s, :, K:], NT, EXACT)
    out_ref[...] = total


def on_device(genotypes, block_units, sketch_seed):
    ind_count = lax.axis_size("ind")
    blk_count = lax.axis_size("blk")
    rows, span = genotypes.shape
    people = rows * ind_count
    own = span // ind_count
    slots = (own // UNIT + MIN_UNITS - 2) // MIN_UNITS + 1
    reach = -(-(MAX_UNITS - 1) // (span // UNIT))
    vmem = pl.BlockSpec(memory_space=pltpu.VMEM)
    smem = pl.BlockSpec(memory_space=pltpu.SMEM)
    wide = people + K
    gram, proj = pl.pallas_call(
        functools.partial(gram_kernel, ind_count, blk_count, slots, reach),
        out_shape=(
            jax.ShapeDtypeStruct((slots, K, K), jnp.float32),
            jax.ShapeDtypeStruct((slots, own, K), jnp.float32),
        ),
        in_specs=[vmem, smem, smem],
        out_specs=(vmem, vmem),
        scratch_shapes=[
            pltpu.VMEM((ind_count, rows, span), jnp.int32),
            pltpu.VMEM((ind_count, 2, span), jnp.float32),
            pltpu.VMEM((2, span), jnp.float32),
            pltpu.VMEM((rows, span), jnp.bfloat16),
            pltpu.VMEM((people, span), jnp.bfloat16),
            pltpu.VMEM((span, K), jnp.bfloat16),
            pltpu.VMEM((2, rows, wide), jnp.float32),
            pltpu.VMEM((2 * reach, rows, wide), jnp.float32),
            pltpu.VMEM((2, ind_count, rows, wide), jnp.float32),
            pltpu.VMEM((slots, people, wide), jnp.float32),
            pltpu.VMEM((slots, K, K), jnp.float32),
            pltpu.VMEM((slots, people, K), jnp.float32),
            pltpu.SemaphoreType.DMA((2, ind_count)),
            pltpu.SemaphoreType.DMA((2, ind_count)),
            pltpu.SemaphoreType.DMA((ind_count,)),
            pltpu.SemaphoreType.DMA((ind_count,)),
            pltpu.SemaphoreType.DMA((2, 2 * reach)),
            pltpu.SemaphoreType.DMA((2, 2 * reach)),
            pltpu.SemaphoreType.DMA((4, ind_count)),
            pltpu.SemaphoreType.DMA((4, ind_count)),
        ],
        compiler_params=pltpu.CompilerParams(
            collective_id=0, has_side_effects=True, vmem_limit_bytes=56 * 2**20
        ),
    )(genotypes, block_units, sketch_seed)
    return pl.pallas_call(
        functools.partial(basis_kernel, slots),
        out_shape=jax.ShapeDtypeStruct((own, K), jnp.float32),
        in_specs=[vmem, pl.BlockSpec(memory_space=pl.ANY)],
        out_specs=vmem,
        scratch_shapes=[
            pltpu.VMEM((slots, K, 2 * K), jnp.float32),
            pltpu.VMEM((slots, own, K), jnp.float32),
            pltpu.SemaphoreType.DMA(()),
        ],
        compiler_params=pltpu.CompilerParams(vmem_limit_bytes=60 * 2**20),
    )(gram, proj)


def solution(mesh):
    return jax.shard_map(
        on_device,
        mesh=mesh,
        in_specs=(P("ind", "blk"), P(), P()),
        out_specs=P(("blk", "ind"), None),
        check_vma=False,
    )
```
